32 devices in a mesh: seq: 4 (over z), chan: 8 (over y, x, core).
Axes of the slice: x: 2, y: 2, z: 4, core: 2. Of those that a mesh axis runs over, the one named last changes fastest.
Arguments:
- query_rows: bfloat16 [16384, 4096], P(('seq', 'chan')), may hold values from -6 to 6
- key_rows: bfloat16 [16384, 4096], P(('seq', 'chan')), may hold values from -6 to 6
- value_rows: bfloat16 [16384, 4096], P(('seq', 'chan')), may hold values from -6 to 6
- residue: float32 [4096, 16], P('chan'), may hold values from -1.5 to 1.5
- pole_rate: float32 [4096, 16], P('chan'), may hold values from 1 to 512
- skip_gain: float32 [4096], P('chan'), may hold values from -4 to 4
- out_weight: bfloat16 [4096, 4096], P('chan', 'seq'), may hold values from -0.09375 to 0.09375
Outputs:
- projected: bfloat16 [4, 4096, 4096], P(None, 'chan', 'seq')
The draws below stay inside these ranges and needn't reach their ends.
All inputs are finite; a program needn't handle non-finite values.
Results may differ from the reference program's by a relative error of at most 0.014.
Values may be sent and summed in bfloat16 or wider, within the bound.
A program may use at most 512 MiB of HBM per device.

```python
import math
import jax
import jax.numpy as jnp
from jax import lax

D = 4096
ORDER = 16
TOK_SEQ = 4096
L = 16384
N_SEQ = 4


def levels(key, dims, shards, smallest, high):
    gain, own = 1.0, jax.random.fold_in(key, 6)
    for axis_at, shards_of in shards:
        draws = jnp.exp(jax.random.uniform(jax.random.fold_in(own, axis_at), (shards_of,), jnp.float32, smallest / len(shards), high / len(shards)))
        gain = gain * jnp.repeat(draws, dims[axis_at] // shards_of).reshape([-1 if axis == axis_at else 1 for axis in range(len(dims))])
    return gain


def scatter_about(stream_key, shape, spread, bound, pieces=(), held_as=jnp.bfloat16):
    result = spread * jax.random.normal(stream_key, shape, jnp.float32)
    if pieces:
        result = result * levels(stream_key, shape, pieces, -0.22, 0.18)
    return jnp.clip(result, -bound, bound).astype(held_as)


def setup_inputs(seed: int = 0) -> dict:
    key_list = jax.random.split(jax.random.key(seed), 8)
    query_rows = scatter_about(key_list[0], (L, D), 1.0, 6.0, ((0, 32),))
    key_rows = scatter_about(key_list[1], (L, D), 1.0, 6.0, ((0, 32),))
    value_rows = scatter_about(key_list[2], (L, D), 1.0, 6.0, ((0, 32),))
    residue = scatter_about(key_list[3], (D, ORDER), 0.25, 1.5, ((0, 8),), jnp.float32)
    pole_rate = jnp.clip(jnp.exp(math.log(512.0) - 6.2383246 * jax.random.uniform(key_list[4], (D, ORDER), jnp.float32) ** levels(key_list[4], (D, ORDER), ((0, 8),), -0.2, 0.2)), 1.0, 512.0)
    skip_gain = scatter_about(key_list[5], (D,), 1.0, 4.0, ((0, 8),), jnp.float32)
    out_weight = scatter_about(key_list[6], (D, D), D ** -0.5, 0.09375, ((0, 8), (1, 4)))
    return dict(query_rows=query_rows, key_rows=key_rows, value_rows=value_rows, residue=residue, pole_rate=pole_rate, skip_gain=skip_gain, out_weight=out_weight)


def filter_response(signal, residue, pole_rate):
    decay_rate = pole_rate / L
    weight = residue * jnp.sqrt(2.0 * decay_rate)
    lag_values = jnp.arange(L, dtype=jnp.float32)[:, None]
    filter_taps = jnp.zeros(signal.shape, jnp.float32)
    for pole_index in range(ORDER):
        filter_taps = filter_taps + weight[:, pole_index][None, :] * jnp.exp(-decay_rate[:, pole_index][None, :] * lag_values)
    padded_len = 2 * L
    spectrum = jnp.fft.rfft(filter_taps, n=padded_len, axis=0) * jnp.fft.rfft(signal, n=padded_len, axis=0)
    return jnp.fft.irfft(spectrum, n=padded_len, axis=0)[:L]

def reference(query_rows, key_rows, value_rows, residue, pole_rate, skip_gain, out_weight):
    product = lax.optimization_barrier((key_rows.astype(jnp.float32) * value_rows.astype(jnp.float32)).astype(jnp.bfloat16))
    signal = product.astype(jnp.float32)
    group_width = math.gcd(D, 256)
    group_count = D // group_width
    grouped = signal.reshape(L, group_count, group_width).transpose(1, 0, 2)
    residue_groups = residue.reshape(group_count, group_width, ORDER)
    rate_groups = pole_rate.reshape(group_count, group_width, ORDER)
    convolved = lax.map(lambda parts: filter_response(parts[0], parts[1], parts[2]), (grouped, residue_groups, rate_groups))
    convolved = convolved.transpose(1, 0, 2).reshape(L, D)
    mixed = lax.optimization_barrier((convolved + skip_gain[None, :] * signal).astype(jnp.bfloat16))
    gated = (query_rows.astype(jnp.float32) * mixed.astype(jnp.float32)).astype(jnp.bfloat16)
    projected = jnp.dot(gated, out_weight, preferred_element_type=jnp.float32).astype(jnp.bfloat16)
    return projected.reshape(N_SEQ, TOK_SEQ, D)
```

```python
import functools

import jax
import jax.numpy as jnp
from jax import lax
from jax.experimental import pallas as pl
from jax.experimental.pallas import tpu as pltpu
from jax.sharding import PartitionSpec as P

LANES = 128
SEGS = 8
PIECES = 4


def block_width(channels):
    return 512 if channels % 512 == 0 else LANES


def tree_sum(terms):
    while len(terms) > 1:
        paired = [terms[i] + terms[i + 1] for i in range(0, len(terms) - 1, 2)]
        if len(terms) % 2:
            paired.append(terms[-1])
        terms = paired
    return terms[0]


def pole_rows(params_ref, lanes, order, length):
    rates = params_ref[order : 2 * order, lanes] / length
    weights = params_ref[0:order, lanes] * jnp.sqrt(2.0 * rates)
    return rates, weights


def spread(row):
    return jnp.broadcast_to(row, (SEGS, LANES))


def load_signal(key_ref, value_ref, lanes, signal_ref):
    product = key_ref[:, lanes].astype(jnp.float32) * value_ref[:, lanes].astype(jnp.float32)
    signal_ref[...] = product.astype(jnp.bfloat16).astype(jnp.float32)


def state_kernel(order, length, params_ref, key_ref, value_ref, ends_ref, final_ref, signal_ref):
    tokens = key_ref.shape[0]
    steps = tokens // SEGS
    behind = (SEGS - 1 - lax.broadcasted_iota(jnp.int32, (SEGS, LANES), 0)).astype(jnp.float32)
    for first in range(0, key_ref.shape[1], LANES):
        lanes = slice(first, first + LANES)
        load_signal(key_ref, value_ref, lanes, signal_ref)
        rates, _ = pole_rows(params_ref, lanes, order, length)
        retain = jnp.exp(-rates)
        factors = [spread(retain[m : m + 1]) for m in range(order)]

        def step(i, states):
            x = signal_ref[pl.ds(i, SEGS, stride=steps), :]
            return tuple(f * s + x for f, s in zip(factors, states))

        zero = jnp.zeros((SEGS, LANES), jnp.float32)
        states = lax.fori_loop(0, steps, step, (zero,) * order, unroll=4)
        for m in range(order):
            ends_ref[m * SEGS : (m + 1) * SEGS, lanes] = states[m]
            carried = states[m] * jnp.exp(-(steps * behind) * spread(rates[m : m + 1]))
            final_ref[m : m + 1, lanes] = jnp.sum(carried, axis=0, keepdims=True)


def output_kernel(
    order,
    length,
    params_ref,
    key_ref,
    value_ref,
    query_ref,
    ends_ref,
    initial_ref,
    gated_ref,
    signal_ref,
    mixed_ref,
):
    tokens = key_ref.shape[0]
    steps = tokens // SEGS
    place = lax.broadcasted_iota(jnp.int32, (SEGS, LANES), 0)
    for first in range(0, key_ref.shape[1], LANES):
        lanes = slice(first, first + LANES)
        load_signal(key_ref, value_ref, lanes, signal_ref)
        rates, weights = pole_rows(params_ref, lanes, order, length)
        retain = jnp.exp(-rates)
        factors = [spread(retain[m : m + 1]) for m in range(order)]
        gains = [spread(weights[m : m + 1]) for m in range(order)]
        direct = spread(params_ref[2 * order : 2 * order + 1, lanes])
        starts = []
        for m in range(order):
            ends = ends_ref[m * SEGS : (m + 1) * SEGS, lanes]
            before = spread(initial_ref[m : m + 1, lanes])
            entry = jnp.where(place == 0, before, pltpu.roll(ends, 1, 0))
            distance = 1
            while distance < SEGS:
                fade = jnp.exp(-float(steps * distance) * spread(rates[m : m + 1]))
                moved = jnp.where(place >= distance, pltpu.roll(entry, distance, 0), 0.0)
                entry = entry + fade * moved
                distance *= 2
            starts.append(entry)

        def step(i, states):
            x = signal_ref[pl.ds(i, SEGS, stride=steps), :]
            states = tuple(f * s + x for f, s in zip(factors, states))
            terms = [g * s for g, s in zip(gains, states)]
            mixed_ref[pl.ds(i, SEGS, stride=steps), :] = tree_sum(terms) + direct * x
            return states

        lax.fori_loop(0, steps, step, tuple(starts), unroll=4)
        mixed = mixed_ref[...].astype(jnp.bfloat16).astype(jnp.float32)
        gated = query_ref[:, lanes].astype(jnp.float32) * mixed
        gated_ref[:, lanes] = gated.astype(jnp.bfloat16)


def copies_to_all(block, axis, count):
    copies = jnp.broadcast_to(block[None], (count,) + block.shape)
    return lax.all_to_all(copies, axis, split_axis=0, concat_axis=0, tiled=True)


def on_device(query_rows, key_rows, value_rows, residue, pole_rate, skip_gain, out_weight):
    tokens, channels = query_rows.shape
    own_channels, order = residue.shape
    seq_count = lax.axis_size("seq")
    chan_count = lax.axis_size("chan")
    length = float(tokens * chan_count * seq_count)

    weight_rows = lax.all_gather(out_weight, "chan", axis=0, tiled=True)

    own_params = jnp.concatenate(
        [residue.T, pole_rate.T, skip_gain[None], jnp.zeros((7, own_channels), jnp.float32)], axis=0
    )
    param_rows = own_params.shape[0]
    params = copies_to_all(own_params, "chan", chan_count)
    params = params.transpose(1, 0, 2).reshape(param_rows, channels)

    width = block_width(channels // PIECES)
    limit = pltpu.CompilerParams(vmem_limit_bytes=40 * 1024 * 1024)
    signal_scratch = pltpu.VMEM((tokens, LANES), jnp.float32)

    def columns(rows, base=0):
        return pl.BlockSpec((rows, width), lambda j: (0, base + j))

    ends, final = pl.pallas_call(
        functools.partial(state_kernel, order, length),
        grid=(channels // width,),
        in_specs=[columns(param_rows), columns(tokens), columns(tokens)],
        out_specs=[columns(order * SEGS), columns(order)],
        out_shape=[
            jax.ShapeDtypeStruct((order * SEGS, channels), jnp.float32),
            jax.ShapeDtypeStruct((order, channels), jnp.float32),
        ],
        scratch_shapes=[signal_scratch],
        compiler_params=limit,
        cost_estimate=pl.CostEstimate(
            flops=2 * order * tokens * channels,
            bytes_accessed=4 * tokens * channels,
            transcendentals=0,
        ),
    )(params, key_rows, value_rows)

    finals = lax.all_to_all(final, "chan", split_axis=1, concat_axis=0, tiled=True)
    finals = finals.reshape(chan_count, order, own_channels)
    rates = pole_rate.T / length
    block_fade = jnp.exp(-rates * tokens)
    total = jnp.zeros((order, own_channels), jnp.float32)
    for j in range(chan_count):
        total = total * block_fade + finals[j]
    totals = copies_to_all(total, "seq", seq_count)
    range_fade = jnp.exp(-rates * (tokens * chan_count))
    own_range = lax.axis_index("seq")
    state = jnp.zeros((order, own_channels), jnp.float32)
    for s in range(seq_count - 1):
        state = jnp.where(s < own_range, state * range_fade + totals[s], state)
    entries = []
    for j in range(chan_count):
        entries.append(state)
        state = state * block_fade + finals[j]
    initial = lax.all_to_all(
        jnp.concatenate(entries, axis=0), "chan", split_axis=0, concat_axis=1, tiled=True
    )
    initial, weight_rows = lax.optimization_barrier((initial, weight_rows))

    piece = channels // PIECES
    result = jnp.zeros((seq_count * tokens, out_weight.shape[1]), jnp.float32)
    for p in range(PIECES):
        base = p * piece // width
        spec = functools.partial(columns, base=base)
        gated = pl.pallas_call(
            functools.partial(output_kernel, order, length),
            grid=(piece // width,),
            in_specs=[
                spec(param_rows),
                spec(tokens),
                spec(tokens),
                spec(tokens),
                spec(order * SEGS),
                spec(order),
            ],
            out_specs=columns(tokens),
            out_shape=jax.ShapeDtypeStruct((tokens, piece), jnp.bfloat16),
            scratch_shapes=[signal_scratch, signal_scratch],
            compiler_params=limit,
            cost_estimate=pl.CostEstimate(
                flops=4 * order * tokens * piece,
                bytes_accessed=8 * tokens * piece,
                transcendentals=0,
            ),
        )(params, key_rows, value_rows, query_rows, ends, initial)
        token_block = lax.all_gather(gated, "seq", axis=0, tiled=True)
        result = result + jnp.dot(
            token_block,
            weight_rows[p * piece : (p + 1) * piece],
            preferred_element_type=jnp.float32,
        )
    return result.astype(jnp.bfloat16).reshape(seq_count, tokens, out_weight.shape[1])


def solution(mesh):
    in_specs = (
        P(("seq", "chan"), None),
        P(("seq", "chan"), None),
        P(("seq", "chan"), None),
        P("chan", None),
        P("chan", None),
        P("chan"),
        P("chan", "seq"),
    )
    out_specs = P(None, "chan", "seq")
    return jax.shard_map(
        on_device, mesh=mesh, in_specs=in_specs, out_specs=out_specs, check_vma=False
    )
```

```python
import functools

import jax
import jax.numpy as jnp
from jax import lax
from jax.experimental import pallas as pl
from jax.experimental.pallas import tpu as pltpu
from jax.sharding import PartitionSpec as P

LANES = 128
SEGS = 8
PIECES = 4


def block_width(channels):
    return 512 if channels % 512 == 0 else LANES


def tree_sum(terms):
    while len(terms) > 1:
        paired = [terms[i] + terms[i + 1] for i in range(0, len(terms) - 1, 2)]
        if len(terms) % 2:
            paired.append(terms[-1])
        terms = paired
    return terms[0]


def pole_rows(params_ref, lanes, order, length):
    rates = params_ref[order : 2 * order, lanes] / length
    weights = params_ref[0:order, lanes] * jnp.sqrt(2.0 * rates)
    return rates, weights


def spread(row):
    return jnp.broadcast_to(row, (SEGS, LANES))


def load_signal(key_ref, value_ref, lanes, signal_ref):
    product = key_ref[:, lanes].astype(jnp.float32) * value_ref[:, lanes].astype(jnp.float32)
    signal_ref[...] = product.astype(jnp.bfloat16).astype(jnp.float32)


def state_kernel(order, length, params_ref, key_ref, value_ref, ends_ref, final_ref, signal_ref):
    tokens = key_ref.shape[0]
    steps = tokens // SEGS
    behind = (SEGS - 1 - lax.broadcasted_iota(jnp.int32, (SEGS, LANES), 0)).astype(jnp.float32)
    for first in range(0, key_ref.shape[1], LANES):
        lanes = slice(first, first + LANES)
        load_signal(key_ref, value_ref, lanes, signal_ref)
        rates, _ = pole_rows(params_ref, lanes, order, length)
        retain = jnp.exp(-rates)
        factors = [spread(retain[m : m + 1]) for m in range(order)]

        def step(i, states):
            x = signal_ref[pl.ds(i, SEGS, stride=steps), :]
            return tuple(f * s + x for f, s in zip(factors, states))

        zero = jnp.zeros((SEGS, LANES), jnp.float32)
        states = lax.fori_loop(0, steps, step, (zero,) * order, unroll=4)
        for m in range(order):
            ends_ref[m * SEGS : (m + 1) * SEGS, lanes] = states[m]
            carried = states[m] * jnp.exp(-(steps * behind) * spread(rates[m : m + 1]))
            final_ref[m : m + 1, lanes] = jnp.sum(carried, axis=0, keepdims=True)


def output_kernel(
    order,
    length,
    params_ref,
    key_ref,
    value_ref,
    query_ref,
    ends_ref,
    initial_ref,
    gated_ref,
    signal_ref,
    mixed_ref,
):
    tokens = key_ref.shape[0]
    steps = tokens // SEGS
    place = lax.broadcasted_iota(jnp.int32, (SEGS, LANES), 0)
    for first in range(0, key_ref.shape[1], LANES):
        lanes = slice(first, first + LANES)
        load_signal(key_ref, value_ref, lanes, signal_ref)
        rates, weights = pole_rows(params_ref, lanes, order, length)
        retain = jnp.exp(-rates)
        factors = [spread(retain[m : m + 1]) for m in range(order)]
        gains = [spread(weights[m : m + 1]) for m in range(order)]
        direct = spread(params_ref[2 * order : 2 * order + 1, lanes])
        starts = []
        for m in range(order):
            ends = ends_ref[m * SEGS : (m + 1) * SEGS, lanes]
            before = spread(initial_ref[m : m + 1, lanes])
            entry = jnp.where(place == 0, before, pltpu.roll(ends, 1, 0))
            distance = 1
            while distance < SEGS:
                fade = jnp.exp(-float(steps * distance) * spread(rates[m : m + 1]))
                moved = jnp.where(place >= distance, pltpu.roll(entry, distance, 0), 0.0)
                entry = entry + fade * moved
                distance *= 2
            starts.append(entry)

        def step(i, states):
            x = signal_ref[pl.ds(i, SEGS, stride=steps), :]
            states = tuple(f * s + x for f, s in zip(factors, states))
            terms = [g * s for g, s in zip(gains, states)]
            mixed_ref[pl.ds(i, SEGS, stride=steps), :] = tree_sum(terms) + direct * x
            return states

        lax.fori_loop(0, steps, step, tuple(starts), unroll=4)
        mixed = mixed_ref[...].astype(jnp.bfloat16).astype(jnp.float32)
        gated = query_ref[:, lanes].astype(jnp.float32) * mixed
        gated_ref[:, lanes] = gated.astype(jnp.bfloat16)


def copies_to_all(block, axis, count):
    copies = jnp.broadcast_to(block[None], (count,) + block.shape)
    return lax.all_to_all(copies, axis, split_axis=0, concat_axis=0, tiled=True)


def on_device(query_rows, key_rows, value_rows, residue, pole_rate, skip_gain, out_weight):
    tokens, channels = query_rows.shape
    own_channels, order = residue.shape
    seq_count = lax.axis_size("seq")
    chan_count = lax.axis_size("chan")
    length = float(tokens * chan_count * seq_count)

    def to_partner(block, distance):
        pairs = [(s, s ^ distance) for s in range(seq_count)]
        return lax.ppermute(block, "seq", pairs)

    weight_own = lax.all_gather(out_weight, "chan", axis=0, tiled=True)
    far_weight = to_partner(out_weight, 2)

    own_params = jnp.concatenate(
        [residue.T, pole_rate.T, skip_gain[None], jnp.zeros((7, own_channels), jnp.float32)], axis=0
    )
    param_rows = own_params.shape[0]
    params = copies_to_all(own_params, "chan", chan_count)
    params = params.transpose(1, 0, 2).reshape(param_rows, channels)

    width = block_width(channels // PIECES)
    limit = pltpu.CompilerParams(vmem_limit_bytes=56 * 1024 * 1024)
    signal_scratch = pltpu.VMEM((tokens, LANES), jnp.float32)

    def columns(rows, base=0):
        return pl.BlockSpec((rows, width), lambda j: (0, base + j))

    ends, final = pl.pallas_call(
        functools.partial(state_kernel, order, length),
        grid=(channels // width,),
        in_specs=[columns(param_rows), columns(tokens), columns(tokens)],
        out_specs=[columns(order * SEGS), columns(order)],
        out_shape=[
            jax.ShapeDtypeStruct((order * SEGS, channels), jnp.float32),
            jax.ShapeDtypeStruct((order, channels), jnp.float32),
        ],
        scratch_shapes=[signal_scratch],
        compiler_params=limit,
        cost_estimate=pl.CostEstimate(
            flops=2 * order * tokens * channels,
            bytes_accessed=4 * tokens * channels,
            transcendentals=0,
        ),
    )(params, key_rows, value_rows)

    finals = lax.all_to_all(final, "chan", split_axis=1, concat_axis=0, tiled=True)
    finals, far_weight = lax.optimization_barrier((finals, far_weight))
    weight_far = lax.all_gather(far_weight, "chan", axis=0, tiled=True)
    finals = finals.reshape(chan_count, order, own_channels)
    rates = pole_rate.T / length
    block_fade = jnp.exp(-rates * tokens)
    total = jnp.zeros((order, own_channels), jnp.float32)
    for j in range(chan_count):
        total = total * block_fade + finals[j]
    totals = copies_to_all(total, "seq", seq_count)
    range_fade = jnp.exp(-rates * (tokens * chan_count))
    own_range = lax.axis_index("seq")
    state = jnp.zeros((order, own_channels), jnp.float32)
    for s in range(seq_count - 1):
        state = jnp.where(s < own_range, state * range_fade + totals[s], state)
    entries = []
    for j in range(chan_count):
        entries.append(state)
        state = state * block_fade + finals[j]
    initial = lax.all_to_all(
        jnp.concatenate(entries, axis=0), "chan", split_axis=0, concat_axis=1, tiled=True
    )
    initial, weight_own = lax.optimization_barrier((initial, weight_own))

    piece = channels // PIECES
    near, partner = [], []
    for p in range(PIECES):
        base = p * piece // width
        spec = functools.partial(columns, base=base)
        gated = pl.pallas_call(
            functools.partial(output_kernel, order, length),
            grid=(piece // width,),
            in_specs=[
                spec(param_rows),
                spec(tokens),
                spec(tokens),
                spec(tokens),
                spec(order * SEGS),
                spec(order),
            ],
            out_specs=columns(tokens),
            out_shape=jax.ShapeDtypeStruct((tokens, piece), jnp.bfloat16),
            scratch_shapes=[signal_scratch, signal_scratch],
            compiler_params=limit,
            cost_estimate=pl.CostEstimate(
                flops=4 * order * tokens * piece,
                bytes_accessed=8 * tokens * piece,
                transcendentals=0,
            ),
        )(params, key_rows, value_rows, query_rows, ends, initial)
        near.append(gated)
        partner.append(to_partner(gated, 1))

    def project(pieces, weight_rows):
        terms = [
            jnp.dot(
                rows,
                weight_rows[p * piece : (p + 1) * piece],
                preferred_element_type=jnp.float32,
            )
            for p, rows in enumerate(pieces)
        ]
        return functools.reduce(jnp.add, terms).astype(jnp.bfloat16)

    blocks = [None] * 4
    blocks[2] = to_partner(project(near, weight_far), 2)
    blocks[3] = to_partner(project(partner, weight_far), 2)
    blocks[0] = project(near, weight_own)
    blocks[1] = project(partner, weight_own)
    result = jnp.zeros((seq_count, tokens, out_weight.shape[1]), jnp.bfloat16)
    for distance, block in enumerate(blocks):
        result = lax.dynamic_update_index_in_dim(result, block, own_range ^ distance, 0)
    return result


def solution(mesh):
    in_specs = (
        P(("seq", "chan"), None),
        P(("seq", "chan"), None),
        P(("seq", "chan"), None),
        P("chan", None),
        P("chan", None),
        P("chan"),
        P("chan", "seq"),
    )
    out_specs = P(None, "chan", "seq")
    return jax.shard_map(
        on_device, mesh=mesh, in_specs=in_specs, out_specs=out_specs, check_vma=False
    )
```
